32 devices in a mesh: tm: 4 (over y, x), height: 8 (over z, core).
Axes of the slice: x: 2, y: 2, z: 4, core: 2. Of those that a mesh axis runs over, the one named last changes fastest.
Arguments:
- queries: bfloat16 [4, 8, 192, 1536], P('tm', 'height'), may hold values from -4.5 to 4.5
- keys: bfloat16 [4, 8, 192, 1536], P('tm', 'height'), may hold values from -4.5 to 4.5
- values: bfloat16 [4, 8, 192, 1536], P('tm', 'height'), may hold values from -6 to 6
- out_grad: bfloat16 [4, 8, 192, 1536], P('tm', 'height'), may hold values from -6 to 6
- tile_counts: int32 [4, 8], replicated, may hold values from 48 to 192, as said below
- clip_ids: int32 [4], replicated, may hold values from 0 to 1, never falling along the last dimension, each value on 1 to 3 neighbouring positions
Outputs:
- query_grad: bfloat16 [4, 8, 192, 1536], P('tm', 'height')
- key_grad: bfloat16 [4, 8, 192, 1536], P('tm', 'height')
- value_grad: bfloat16 [4, 8, 192, 1536], P('tm', 'height')
The draws below stay inside these ranges and needn't reach their ends.
Inputs may be any that keep to these rules, and one draw needn't show every extreme that they name: `tile_counts`: at least a quarter of a tile's slots are valid; some tile is full.
All inputs are finite; a program needn't handle non-finite values.
Results may differ from the reference program's by a relative error of at most 0.0085.
Values may be sent and summed in bfloat16 or wider, within the bound.
A program may use at most 192 MiB of HBM per device.

```python
import math
import jax
import jax.numpy as jnp
import numpy as np
from jax import lax

HEADS = 12
HEAD = 128
TILE = 192
HD = 1536
NTT = 4
NTH = 8
N_TM = 4


def draw_queries(key, part):
    key = jax.random.fold_in(key, 1)
    result = jnp.clip(jax.random.normal(key, (NTT, NTH, TILE, HD), jnp.float32), -4.5, 4.5)
    return result.astype(jnp.bfloat16)


def draw_keys(key, part):
    key = jax.random.fold_in(key, 2)
    result = jnp.clip(jax.random.normal(key, (NTT, NTH, TILE, HD), jnp.float32), -4.5, 4.5)
    return result.astype(jnp.bfloat16)


def draw_tile_counts(key, part):
    key = jax.random.fold_in(key, 3)
    counts = jax.random.randint(jax.random.fold_in(key, 1), (NTT, NTH), TILE // 4, TILE + 1)
    chosen = jax.random.randint(jax.random.fold_in(key, 2), (), 0, NTT * NTH)
    places = jnp.arange(NTT * NTH, dtype=jnp.int32).reshape(NTT, NTH)
    return jnp.where(places == chosen, TILE, counts).astype(jnp.int32)


def level_of(rng, shape, split, smallest, largest):
    gain = 1.0
    for dim, shards_of in split:
        steps = jax.random.uniform(jax.random.fold_in(jax.random.fold_in(rng, 6), dim), (shards_of,), jnp.float32, smallest / len(split), largest / len(split))
        gain = gain * jnp.repeat(jnp.exp(steps), shape[dim] // shards_of).reshape((-1,) + (1,) * (len(shape) - 1 - dim))
    return gain


def split_up(number_of, total, most, slope):
    weights = [(1 << 20) // math.isqrt(standing ** slope) + 1 for standing in range(2, number_of + 1)]
    spare, given = total - most - (number_of - 1), [1] * (number_of - 1)
    while spare > 0:
        free = [i for i in range(number_of - 1) if given[i] < most]
        pool, left = sum([weights[i] for i in free]), spare
        for i in free:
            addition = min(most - given[i], max(1, left * weights[i] // pool), spare)
            given[i] = given[i] + addition
            spare = spare - addition
    return np.array([most] + given)


def ragged(own_key, count, total, limit, skew):
    if count == 2:
        one = jax.random.randint(own_key, (), max(1, total - limit), min(limit, total - 1) + 1)
        return jnp.stack([one, total - one])
    tallies = jnp.asarray(split_up(count, total, limit, skew), jnp.int32)
    twos = (count - 1) // 2
    donor, receiver = tallies[1:1 + 2 * twos:2], tallies[2:2 + 2 * twos:2]
    margin = jnp.minimum(donor - 1, limit - receiver)
    passed = jax.random.randint(jax.random.fold_in(own_key, 1), (twos,), 0, 1 << 20) % (margin + 1)
    tallies = tallies.at[1:1 + 2 * twos:2].set(donor - passed).at[2:2 + 2 * twos:2].set(receiver + passed)
    return tallies[jax.random.permutation(jax.random.fold_in(own_key, 2), count)]


def normal_values(rng, extent, spread, most, cuts=(), kind=jnp.bfloat16):
    level = level_of(rng, extent, cuts, -0.22, 0.18) if cuts else 1.0
    drawn = jax.random.normal(rng, extent, jnp.float32) * spread * level
    return jnp.minimum(jnp.maximum(drawn, -most), most).astype(kind)


def setup_inputs(seed: int = 0) -> dict:
    key_list = jax.random.split(jax.random.key(seed), 7)
    queries = draw_queries(jax.random.fold_in(key_list[6], 71), 0)
    keys = draw_keys(jax.random.fold_in(key_list[6], 71), 0)
    values = normal_values(key_list[2], (NTT, NTH, TILE, HD), 1.0, 6.0, ((0, 4), (1, 8)))
    out_grad = normal_values(key_list[3], (NTT, NTH, TILE, HD), 1.0, 6.0, ((0, 4), (1, 8)))
    tile_counts = draw_tile_counts(jax.random.fold_in(key_list[6], 71), 0)
    clip_ids = jnp.searchsorted(jnp.cumsum(ragged(key_list[5], N_TM // 2, NTT, 3, 0)), jnp.arange(NTT), side="right").astype(jnp.int32)
    return {"queries": queries, "keys": keys, "values": values, "out_grad": out_grad, "tile_counts": tile_counts, "clip_ids": clip_ids}


def window_mask(tile_counts, clip_ids, row, col):
    n_time = tile_counts.shape[0]
    n_high = tile_counts.shape[1]
    offsets = jnp.arange(3, dtype=jnp.int32) - 1
    along_t = row + offsets
    along_h = col + offsets
    inside = ((along_t >= 0) & (along_t < n_time))[:, None] & ((along_h >= 0) & (along_h < n_high))[None, :]
    clamp_t = jnp.clip(along_t, 0, n_time - 1)
    clamp_h = jnp.clip(along_h, 0, n_high - 1)
    rows_all = jnp.arange(n_time, dtype=jnp.int32)
    cols_all = jnp.arange(n_high, dtype=jnp.int32)
    hits = (clamp_t[:, None, None, None] == rows_all[None, None, :, None]) & (clamp_h[None, :, None, None] == cols_all[None, None, None, :])
    counts = jnp.sum(jnp.where(hits, tile_counts[None, None], 0), axis=(2, 3))
    clip_near = jnp.sum(jnp.where(clamp_t[:, None] == rows_all[None, :], clip_ids[None, :], 0), axis=1)
    same = clip_near == clip_near[1]
    slots = jnp.arange(TILE, dtype=jnp.int32)
    return inside[:, :, None] & same[:, None, None] & (slots[None, None, :] < counts[:, :, None])


def tile_grads(query, key_win, value_win, cotangent, key_mask, query_mask):
    scale = 1.0 / (HEAD ** 0.5)
    q_heads = query.reshape(TILE, HEADS, HEAD).astype(jnp.float32)
    k_heads = key_win.reshape(-1, HEADS, HEAD).astype(jnp.float32)
    v_heads = value_win.reshape(-1, HEADS, HEAD).astype(jnp.float32)
    g_heads = cotangent.reshape(TILE, HEADS, HEAD).astype(jnp.float32)
    scores = jnp.einsum("qhd,khd->hqk", q_heads, k_heads) * scale
    scores = jnp.where(key_mask[None, None, :], scores, jnp.float32(-1e30))
    top = jnp.max(scores, axis=-1, keepdims=True)
    lse = top + jnp.log(jnp.sum(jnp.exp(scores - top), axis=-1, keepdims=True))
    probs = jnp.exp(scores - lse) * query_mask[None, :, None].astype(jnp.float32)
    probs_b = lax.optimization_barrier(probs.astype(jnp.bfloat16)).astype(jnp.float32)
    attended = jnp.einsum("hqk,khd->qhd", probs_b, v_heads)
    delta = jnp.einsum("qhd,qhd->hq", g_heads, attended)
    prob_grad = jnp.einsum("qhd,khd->hqk", g_heads, v_heads)
    score_grad = (probs * (prob_grad - delta[:, :, None])).astype(jnp.bfloat16)
    score_grad = lax.optimization_barrier(score_grad).astype(jnp.float32)
    dquery = (jnp.einsum("hqk,khd->qhd", score_grad, k_heads) * scale).reshape(TILE, HD)
    dkey = (jnp.einsum("hqk,qhd->khd", score_grad, q_heads) * scale).reshape(-1, HD)
    dvalue = jnp.einsum("hqk,qhd->khd", probs_b, g_heads).reshape(-1, HD)
    dkey = lax.optimization_barrier(dkey.astype(jnp.bfloat16)).astype(jnp.float32)
    dvalue = lax.optimization_barrier(dvalue.astype(jnp.bfloat16)).astype(jnp.float32)
    return dquery.astype(jnp.bfloat16), dkey, dvalue


def reference(queries, keys, values, out_grad, tile_counts, clip_ids):
    padding = ((1, 1), (1, 1), (0, 0), (0, 0))
    pad_keys = jnp.pad(keys, padding)
    pad_values = jnp.pad(values, padding)
    zero = jnp.zeros((), jnp.int32)
    acc_shape = (NTT + 2, NTH + 2, TILE, HD)

    def step(index, carry):
        dq_all, acc_k, acc_v = carry
        index = jnp.asarray(index).astype(jnp.int32)
        row = (index // NTH).astype(jnp.int32)
        col = (index % NTH).astype(jnp.int32)
        start = (row, col, zero, zero)
        key_win = lax.dynamic_slice(pad_keys, start, (3, 3, TILE, HD)).reshape(9 * TILE, HD)
        value_win = lax.dynamic_slice(pad_values, start, (3, 3, TILE, HD)).reshape(9 * TILE, HD)
        query = lax.dynamic_slice(queries, start, (1, 1, TILE, HD)).reshape(TILE, HD)
        cotangent = lax.dynamic_slice(out_grad, start, (1, 1, TILE, HD)).reshape(TILE, HD)
        visible = window_mask(tile_counts, clip_ids, row, col)
        dquery, dkey, dvalue = tile_grads(query, key_win, value_win, cotangent, visible.reshape(-1), visible[1, 1])
        dq_all = lax.dynamic_update_slice(dq_all, dquery.reshape(1, 1, TILE, HD), start)
        acc_k = lax.dynamic_update_slice(acc_k, lax.dynamic_slice(acc_k, start, (3, 3, TILE, HD)) + dkey.reshape(3, 3, TILE, HD), start)
        acc_v = lax.dynamic_update_slice(acc_v, lax.dynamic_slice(acc_v, start, (3, 3, TILE, HD)) + dvalue.reshape(3, 3, TILE, HD), start)
        return dq_all, acc_k, acc_v

    init = (jnp.zeros(queries.shape, jnp.bfloat16), jnp.zeros(acc_shape, jnp.float32), jnp.zeros(acc_shape, jnp.float32))
    dq_all, acc_k, acc_v = lax.fori_loop(0, NTT * NTH, step, init)
    return dq_all, acc_k[1:-1, 1:-1].astype(jnp.bfloat16), acc_v[1:-1, 1:-1].astype(jnp.bfloat16)
```

```python
import functools
import math

import jax
import jax.numpy as jnp
from jax import lax
from jax.experimental import pallas as pl
from jax.experimental.pallas import tpu as pltpu
from jax.sharding import PartitionSpec as P

HEADS = 12
HEAD = 128
TILE = 192
HD = 1536
MESH = pl.DeviceIdType.MESH
SCALE = 1.0 / HEAD**0.5
ROWS = 4
PER = HEADS // ROWS
WIN = 9


def head_kernel(
    n_high,
    counts,
    clips,
    q_in,
    k_in,
    v_in,
    g_in,
    dq_out,
    dk_out,
    dv_out,
    kv,
    qg,
    score,
    pgrad,
    dq_t,
    acc,
    t_send,
    t_recv,
    o_send,
    in_send,
    in_recv,
    kv_send,
    kv_recv,
    tr_send,
    tr_recv,
    out_send,
    out_recv,
):
    me = lax.axis_index("tm")
    col = lax.axis_index("height")
    has_low = col > 0
    has_high = col < n_high - 1
    peers = [lax.rem(me + i, ROWS) for i in (1, 2, 3)]

    barrier = pltpu.get_barrier_semaphore()
    for peer in peers:
        pl.semaphore_signal(barrier, inc=1, device_id=(peer, col), device_id_type=MESH)

    @pl.when(has_low)
    def _():
        pl.semaphore_signal(barrier, inc=1, device_id=(me, col - 1), device_id_type=MESH)

    @pl.when(has_high)
    def _():
        pl.semaphore_signal(barrier, inc=1, device_id=(me, col + 1), device_id_type=MESH)

    pl.semaphore_wait(barrier, 3 + has_low.astype(jnp.int32) + has_high.astype(jnp.int32))

    sources = (k_in, v_in, q_in, g_in)

    def landing(j, a, r):
        return kv.at[j, 1, a, r] if a < 2 else qg.at[j, a - 2, r]

    def in_copy(j, a, peer):
        start = pl.multiple_of((peer * PER + j) * HEAD, HEAD)
        return pltpu.make_async_remote_copy(
            src_ref=sources[a].at[0, 0, :, pl.ds(start, HEAD)],
            dst_ref=landing(j, a, me),
            send_sem=in_send.at[j, a, peer],
            recv_sem=in_recv.at[j, a, me],
            device_id=(peer, col),
            device_id_type=MESH,
        )

    def in_local(j, a):
        start = pl.multiple_of((me * PER + j) * HEAD, HEAD)
        return pltpu.make_async_copy(
            sources[a].at[0, 0, :, pl.ds(start, HEAD)], landing(j, a, me), in_recv.at[j, a, me]
        )

    def in_arrival(j, a, peer):
        return pltpu.make_async_remote_copy(
            src_ref=landing(j, a, peer),
            dst_ref=landing(j, a, peer),
            send_sem=in_send.at[j, a, peer],
            recv_sem=in_recv.at[j, a, peer],
            device_id=(peer, col),
            device_id_type=MESH,
        )

    def start_in(j, _):
        for a in range(4):
            for peer in (peers[1], peers[0], peers[2]):
                in_copy(j, a, peer).start()
            in_local(j, a).start()
        return 0

    lax.fori_loop(0, PER, start_in, 0)

    def wait_in(j, arrays):
        for a in arrays:
            in_local(j, a).wait()
            for peer in peers:
                in_arrival(j, a, peer).wait_recv()

    sides = ((0, has_low, -1), (1, has_high, 1))

    def kv_copy(j, side, step):
        return pltpu.make_async_remote_copy(
            src_ref=kv.at[j, 1],
            dst_ref=kv.at[j, 2 - 2 * side],
            send_sem=kv_send.at[j, side],
            recv_sem=kv_recv.at[j, 1 - side],
            device_id=(me, col + step),
            device_id_type=MESH,
        )

    def kv_arrival(j, side, step):
        return pltpu.make_async_remote_copy(
            src_ref=kv.at[j, 1],
            dst_ref=kv.at[j, 2 * side],
            send_sem=kv_send.at[j, side],
            recv_sem=kv_recv.at[j, side],
            device_id=(me, col + step),
            device_id_type=MESH,
        )

    def term_copy(j, side, step):
        return pltpu.make_async_remote_copy(
            src_ref=t_send.at[j, side],
            dst_ref=t_recv.at[j, 1 - side],
            send_sem=tr_send.at[j, side],
            recv_sem=tr_recv.at[j, 1 - side],
            device_id=(me, col + step),
            device_id_type=MESH,
        )

    def term_arrival(j, side, step):
        return pltpu.make_async_remote_copy(
            src_ref=t_send.at[j, side],
            dst_ref=t_recv.at[j, side],
            send_sem=tr_send.at[j, side],
            recv_sem=tr_recv.at[j, side],
            device_id=(me, col + step),
            device_id_type=MESH,
        )

    def forward(j):
        wait_in(j, (0, 1))
        for side, there, step in sides:

            @pl.when(there)
            def _():
                kv_copy(j, side, step).start()

            @pl.when(jnp.logical_not(there))
            def _():
                kv[j, 2 * side] = jnp.zeros((2, ROWS, TILE, HEAD), jnp.bfloat16)

    results = (dq_out, dk_out, dv_out)

    def out_place(j, o, row):
        start = pl.multiple_of((row * PER + j) * HEAD, HEAD)
        return results[o].at[0, 0, :, pl.ds(start, HEAD)]

    def out_copy(j, o, peer):
        return pltpu.make_async_remote_copy(
            src_ref=o_send.at[j, o, peer],
            dst_ref=out_place(j, o, me),
            send_sem=out_send.at[j, o, peer],
            recv_sem=out_recv.at[j, o, me],
            device_id=(peer, col),
            device_id_type=MESH,
        )

    def out_local(j, o):
        return pltpu.make_async_copy(
            o_send.at[j, o, me], out_place(j, o, me), out_send.at[j, o, me]
        )

    def out_arrival(j, o, peer):
        return pltpu.make_async_remote_copy(
            src_ref=o_send.at[j, o, peer],
            dst_ref=out_place(j, o, peer),
            send_sem=out_send.at[j, o, peer],
            recv_sem=out_recv.at[j, o, peer],
            device_id=(peer, col),
            device_id_type=MESH,
        )

    def start_out(j, o):
        for peer in (peers[1], peers[0], peers[2]):
            out_copy(j, o, peer).start()
        out_local(j, o).start()

    lane = lax.broadcasted_iota(jnp.int32, (1, 2 * TILE), 1)
    first_half = lane < TILE
    slot = lax.broadcasted_iota(jnp.int32, (TILE, 2 * TILE), 0)

    def visible_count(row, key_row, offset):
        there = col + offset - 1
        inside = (there >= 0) & (there < n_high)
        near = jnp.abs(row - key_row) <= 1
        same = clips[row] == clips[key_row]
        count = counts[key_row, jnp.clip(there, 0, n_high - 1)]
        return jnp.where(inside & near & same, count, 0)

    def fold(x, op):
        return op(x.reshape(TILE // 8, 8, 2 * TILE), axis=0)

    def block(j, b):
        row = 2 * b
        q = qg[j, 0, pl.ds(row, 2)].reshape(2 * TILE, HEAD)
        g = qg[j, 1, pl.ds(row, 2)].reshape(2 * TILE, HEAD)
        q_t = q.T
        g_t = g.T

        def scores(t, top):
            key_row, offset = b + t // 3, t % 3
            s = jnp.dot(kv[j, offset, 0, key_row], q_t, preferred_element_type=jnp.float32)
            limit = jnp.where(
                first_half,
                visible_count(row, key_row, offset),
                visible_count(row + 1, key_row, offset),
            )
            s = jnp.where(slot < limit, s * (SCALE * math.log2(math.e)), jnp.float32(-1e30))
            score[t] = s
            pgrad[t] = jnp.dot(kv[j, offset, 1, key_row], g_t, preferred_element_type=jnp.float32)
            return jnp.maximum(top, fold(s, jnp.max))

        top = lax.fori_loop(0, WIN, scores, jnp.full((8, 2 * TILE), -1e30, jnp.float32))
        top = jnp.max(top, axis=0, keepdims=True)

        def sums(t, carry):
            total, dot = carry
            e = jnp.exp2(score[t] - top)
            score[t] = e
            return total + fold(e, jnp.sum), dot + fold(e * pgrad[t], jnp.sum)

        zero = jnp.zeros((8, 2 * TILE), jnp.float32)
        total, dot = lax.fori_loop(0, WIN, sums, (zero, zero))
        total = jnp.sum(total, axis=0, keepdims=True)
        dot = jnp.sum(dot, axis=0, keepdims=True)
        own = jnp.where(first_half, counts[row, col], counts[row + 1, col] + TILE)
        inverse = 1.0 / total
        delta = dot * inverse
        inverse = jnp.where(lane < own, inverse, 0.0)
        dq_t[...] = jnp.zeros_like(dq_t)

        def grads(t, _):
            key_row, offset = b + t // 3, t % 3
            p = score[t] * inverse
            ds = (p * (pgrad[t] - delta)).astype(jnp.bfloat16)
            p = p.astype(jnp.bfloat16)
            k_t = kv[j, offset, 0, key_row].T
            dq_t[...] += jnp.dot(k_t, ds, preferred_element_type=jnp.float32)
            fresh = (b == 0) | (key_row == ROWS - 1)
            old_k = jnp.where(fresh, 0.0, acc[j, offset, 0, key_row])
            acc[j, offset, 0, key_row] = old_k + jnp.dot(ds, q, preferred_element_type=jnp.float32)
            old_v = jnp.where(fresh, 0.0, acc[j, offset, 1, key_row])
            acc[j, offset, 1, key_row] = old_v + jnp.dot(p, g, preferred_element_type=jnp.float32)
            return 0

        lax.fori_loop(0, WIN, grads, 0)
        dq = (dq_t[...] * SCALE).T.astype(jnp.bfloat16)
        o_send[j, 0, pl.ds(row, 2)] = dq.reshape(2, TILE, HEAD)

    def send_terms(j):
        for side, there, step in sides:

            @pl.when(there)
            def _():
                def cast(r, _):
                    t_send[j, side, 0, r] = (acc[j, 2 * side, 0, r] * SCALE).astype(jnp.bfloat16)
                    t_send[j, side, 1, r] = acc[j, 2 * side, 1, r].astype(jnp.bfloat16)
                    return 0

                lax.fori_loop(0, ROWS, cast, 0)
                term_copy(j, side, step).start()

    def finish(j):
        for side, there, step in sides:

            @pl.when(there)
            def _():
                term_arrival(j, side, step).wait_recv()

            @pl.when(jnp.logical_not(there))
            def _():
                t_recv[j, side] = jnp.zeros((2, ROWS, TILE, HEAD), jnp.bfloat16)

        def add(r, _):
            dk = (
                acc[j, 1, 0, r] * SCALE
                + t_recv[j, 0, 0, r].astype(jnp.float32)
                + t_recv[j, 1, 0, r].astype(jnp.float32)
            )
            dv = (
                acc[j, 1, 1, r]
                + t_recv[j, 0, 1, r].astype(jnp.float32)
                + t_recv[j, 1, 1, r].astype(jnp.float32)
            )
            o_send[j, 1, r] = dk.astype(jnp.bfloat16)
            o_send[j, 2, r] = dv.astype(jnp.bfloat16)
            return 0

        lax.fori_loop(0, ROWS, add, 0)
        start_out(j, 1)
        start_out(j, 2)

    forward(0)

    def head(j, _):
        @pl.when(j + 1 < PER)
        def _():
            forward(j + 1)

        wait_in(j, (2, 3))
        for side, there, step in sides:

            @pl.when(there)
            def _():
                kv_arrival(j, side, step).wait_recv()

        def one_block(b, _):
            block(j, b)
            return 0

        lax.fori_loop(0, ROWS // 2, one_block, 0)
        send_terms(j)
        start_out(j, 0)

        @pl.when(j > 0)
        def _():
            finish(j - 1)

        return 0

    lax.fori_loop(0, PER, head, 0)
    finish(PER - 1)

    def drain(j, _):
        for a in range(4):
            for peer in peers:
                in_copy(j, a, peer).wait_send()
        for side, there, step in sides:

            @pl.when(there)
            def _():
                kv_copy(j, side, step).wait_send()
                term_copy(j, side, step).wait_send()

        for o in range(3):
            out_local(j, o).wait()
            for peer in peers:
                out_copy(j, o, peer).wait_send()
                out_arrival(j, o, peer).wait_recv()
        return 0

    lax.fori_loop(0, PER, drain, 0)


def by_heads(n_high, queries, keys, values, out_grad, tile_counts, clip_ids):
    tile = (TILE, HEAD)
    shape = jax.ShapeDtypeStruct(queries.shape, jnp.bfloat16)
    bf16, f32 = jnp.bfloat16, jnp.float32
    dma = pltpu.SemaphoreType.DMA
    pairs = 10 * 3 * PER
    return tuple(
        pl.pallas_call(
            functools.partial(head_kernel, n_high),
            out_shape=(shape, shape, shape),
            in_specs=[pl.BlockSpec(memory_space=pltpu.SMEM)] * 2
            + [pl.BlockSpec(memory_space=pl.ANY)] * 4,
            out_specs=(pl.BlockSpec(memory_space=pl.ANY),) * 3,
            scratch_shapes=[
                pltpu.VMEM((PER, 3, 2, ROWS) + tile, bf16),
                pltpu.VMEM((PER, 2, ROWS) + tile, bf16),
                pltpu.VMEM((WIN, TILE, 2 * TILE), f32),
                pltpu.VMEM((WIN, TILE, 2 * TILE), f32),
                pltpu.VMEM((HEAD, 2 * TILE), f32),
                pltpu.VMEM((PER, 3, 2, ROWS) + tile, f32),
                pltpu.VMEM((PER, 2, 2, ROWS) + tile, bf16),
                pltpu.VMEM((PER, 2, 2, ROWS) + tile, bf16),
                pltpu.VMEM((PER, 3, ROWS) + tile, bf16),
                dma((PER, 4, ROWS)),
                dma((PER, 4, ROWS)),
                dma((PER, 2)),
                dma((PER, 2)),
                dma((PER, 2)),
                dma((PER, 2)),
                dma((PER, 3, ROWS)),
                dma((PER, 3, ROWS)),
            ],
            compiler_params=pltpu.CompilerParams(
                collective_id=0, has_side_effects=True, vmem_limit_bytes=48 * 1024 * 1024
            ),
            cost_estimate=pl.CostEstimate(
                flops=pairs * 5 * 2 * TILE * TILE * HEAD,
                bytes_accessed=7 * TILE * HD * 2,
                transcendentals=pairs * TILE * TILE,
            ),
            name="head_parallel",
        )(tile_counts, clip_ids, queries, keys, values, out_grad)
    )


def extended(block, sides, width):
    for axis, dim in sides:
        count = lax.axis_size(axis)
        forward = [(i, i + 1) for i in range(count - 1)]
        backward = [(target, source) for source, target in forward]
        low = lax.ppermute(
            lax.slice_in_dim(block, block.shape[dim] - width, None, axis=dim), axis, forward
        )
        high = lax.ppermute(lax.slice_in_dim(block, 0, width, axis=dim), axis, backward)
        block = jnp.concatenate([low, block, high], axis=dim)
    return block


def window_mask(tile_counts, clip_ids, row, col):
    n_time = tile_counts.shape[0]
    n_high = tile_counts.shape[1]
    offsets = jnp.arange(3, dtype=jnp.int32) - 1
    along_t = row + offsets
    along_h = col + offsets
    inside = ((along_t >= 0) & (along_t < n_time))[:, None] & ((along_h >= 0) & (along_h < n_high))[
        None, :
    ]
    clamp_t = jnp.clip(along_t, 0, n_time - 1)
    clamp_h = jnp.clip(along_h, 0, n_high - 1)
    rows_all = jnp.arange(n_time, dtype=jnp.int32)
    cols_all = jnp.arange(n_high, dtype=jnp.int32)
    hits = (clamp_t[:, None, None, None] == rows_all[None, None, :, None]) & (
        clamp_h[None, :, None, None] == cols_all[None, None, None, :]
    )
    counts = jnp.sum(jnp.where(hits, tile_counts[None, None], 0), axis=(2, 3))
    clip_near = jnp.sum(
        jnp.where(clamp_t[:, None] == rows_all[None, :], clip_ids[None, :], 0), axis=1
    )
    same = clip_near == clip_near[1]
    slots = jnp.arange(TILE, dtype=jnp.int32)
    return inside[:, :, None] & same[:, None, None] & (slots[None, None, :] < counts[:, :, None])


def query_side(query, key_win, value_win, cotangent, key_mask, query_mask):
    scale = 1.0 / HEAD**0.5
    q_heads = query.reshape(TILE, HEADS, HEAD)
    k_heads = key_win.reshape(-1, HEADS, HEAD)
    v_heads = value_win.reshape(-1, HEADS, HEAD)
    g_heads = cotangent.reshape(TILE, HEADS, HEAD)
    scores = (
        jnp.einsum("qhd,khd->hqk", q_heads, k_heads, preferred_element_type=jnp.float32) * scale
    )
    scores = jnp.where(key_mask[None, None, :], scores, jnp.float32(-1e30))
    top = jnp.max(scores, axis=-1, keepdims=True)
    lse = top + jnp.log(jnp.sum(jnp.exp(scores - top), axis=-1, keepdims=True))
    probs = jnp.exp(scores - lse) * query_mask[None, :, None].astype(jnp.float32)
    probs_b = probs.astype(jnp.bfloat16)
    attended = jnp.einsum("hqk,khd->qhd", probs_b, v_heads, preferred_element_type=jnp.float32)
    delta = jnp.einsum("qhd,qhd->hq", g_heads.astype(jnp.float32), attended)
    prob_grad = jnp.einsum("qhd,khd->hqk", g_heads, v_heads, preferred_element_type=jnp.float32)
    score_grad = (probs * (prob_grad - delta[:, :, None])).astype(jnp.bfloat16)
    dquery = (
        jnp.einsum("hqk,khd->qhd", score_grad, k_heads, preferred_element_type=jnp.float32) * scale
    ).reshape(TILE, HD)
    dquery = dquery.astype(jnp.bfloat16)
    return (dquery, lse[:, :, 0], delta)


def local(queries, keys, values, out_grad, tile_counts, clip_ids):
    row = lax.axis_index("tm")
    col = lax.axis_index("height")
    visible = window_mask(tile_counts, clip_ids, row, col)
    own_mask = visible[1, 1]
    query = queries.reshape(TILE, HD)
    cotangent = out_grad.reshape(TILE, HD)
    windowed = extended(jnp.stack([keys, values]), (("tm", 1), ("height", 2)), 1)
    key_win = windowed[0].reshape(9 * TILE, HD)
    value_win = windowed[1].reshape(9 * TILE, HD)
    shape_out = (1, 1, TILE, HD)
    near = extended(jnp.stack([queries, out_grad]), (("tm", 1), ("height", 2)), 1)
    dquery, lse, delta = query_side(
        query, key_win, value_win, cotangent, visible.reshape(-1), own_mask
    )
    stats = extended(jnp.stack([lse, delta])[:, None, None], (("tm", 1), ("height", 2)), 1)
    lse_near = stats[0].transpose(2, 0, 1, 3).reshape(HEADS, 9 * TILE)
    delta_near = stats[1].transpose(2, 0, 1, 3).reshape(HEADS, 9 * TILE)
    scale = 1.0 / HEAD**0.5
    q_near = near[0].reshape(9 * TILE, HEADS, HEAD)
    g_near = near[1].reshape(9 * TILE, HEADS, HEAD)
    k_own = keys.reshape(TILE, HEADS, HEAD)
    v_own = values.reshape(TILE, HEADS, HEAD)
    pair_mask = visible.reshape(-1)[:, None] & own_mask[None, :]
    scores = jnp.einsum("qhd,khd->hqk", q_near, k_own, preferred_element_type=jnp.float32) * scale
    probs = jnp.where(pair_mask[None], jnp.exp(scores - lse_near[:, :, None]), jnp.float32(0.0))
    probs_b = probs.astype(jnp.bfloat16)
    prob_grad = jnp.einsum("qhd,khd->hqk", g_near, v_own, preferred_element_type=jnp.float32)
    score_grad = (probs * (prob_grad - delta_near[:, :, None])).astype(jnp.bfloat16)
    score_tiles = score_grad.reshape(HEADS, 9, TILE, TILE)
    probs_tiles = probs_b.reshape(HEADS, 9, TILE, TILE)
    q_tiles = q_near.reshape(9, TILE, HEADS, HEAD)
    g_tiles = g_near.reshape(9, TILE, HEADS, HEAD)
    key_terms = (
        jnp.einsum("hnqk,nqhd->nkhd", score_tiles, q_tiles, preferred_element_type=jnp.float32)
        * scale
    ).astype(jnp.bfloat16)
    value_terms = jnp.einsum(
        "hnqk,nqhd->nkhd", probs_tiles, g_tiles, preferred_element_type=jnp.float32
    ).astype(jnp.bfloat16)
    dkey = jnp.sum(key_terms.astype(jnp.float32), axis=0)
    dvalue = jnp.sum(value_terms.astype(jnp.float32), axis=0)
    key_grad = dkey.reshape(shape_out).astype(jnp.bfloat16)
    value_grad = dvalue.reshape(shape_out).astype(jnp.bfloat16)
    return (dquery.reshape(shape_out), key_grad, value_grad)


def solution(mesh):
    placed = (
        P("tm", "height", None, None),
        P("tm", "height", None, None),
        P("tm", "height", None, None),
        P("tm", "height", None, None),
        P(),
        P(),
    )
    if mesh.shape["tm"] == ROWS:
        body = functools.partial(by_heads, mesh.shape["height"])
    else:
        body = local
    return jax.shard_map(
        body,
        mesh=mesh,
        in_specs=placed,
        out_specs=(
            P("tm", "height", None, None),
            P("tm", "height", None, None),
            P("tm", "height", None, None),
        ),
        check_vma=False,
    )
```

```python
import functools
import math

import jax
import jax.numpy as jnp
from jax import lax
from jax.experimental import pallas as pl
from jax.experimental.pallas import tpu as pltpu
from jax.sharding import PartitionSpec as P

HEADS = 12
HEAD = 128
TILE = 192
HD = 1536
MESH = pl.DeviceIdType.MESH
SCALE = 1.0 / HEAD**0.5
ROWS = 4
PER = HEADS // ROWS
WIN = 9


def head_kernel(
    n_high,
    counts,
    clips,
    q_in,
    k_in,
    v_in,
    g_in,
    dq_out,
    dk_out,
    dv_out,
    kv,
    qg,
    score,
    pgrad,
    dq_t,
    acc,
    t_send,
    t_recv,
    o_send,
    in_send,
    in_recv,
    kv_send,
    kv_recv,
    tr_send,
    tr_recv,
    out_send,
    out_recv,
):
    me = lax.axis_index("tm")
    col = lax.axis_index("height")
    has_low = col > 0
    has_high = col < n_high - 1
    peers = [lax.rem(me + i, ROWS) for i in (1, 2, 3)]

    barrier = pltpu.get_barrier_semaphore()
    for peer in peers:
        pl.semaphore_signal(barrier, inc=1, device_id=(peer, col), device_id_type=MESH)

    @pl.when(has_low)
    def _():
        pl.semaphore_signal(barrier, inc=1, device_id=(me, col - 1), device_id_type=MESH)

    @pl.when(has_high)
    def _():
        pl.semaphore_signal(barrier, inc=1, device_id=(me, col + 1), device_id_type=MESH)

    pl.semaphore_wait(barrier, 3 + has_low.astype(jnp.int32) + has_high.astype(jnp.int32))

    sources = (k_in, v_in, q_in, g_in)

    def landing(j, a, r):
        return kv.at[j, 1, a, r] if a < 2 else qg.at[j, a - 2, r]

    def in_copy(j, a, peer):
        start = pl.multiple_of((peer * PER + j) * HEAD, HEAD)
        return pltpu.make_async_remote_copy(
            src_ref=sources[a].at[0, 0, :, pl.ds(start, HEAD)],
            dst_ref=landing(j, a, me),
            send_sem=in_send.at[j, a, peer],
            recv_sem=in_recv.at[j, a, me],
            device_id=(peer, col),
            device_id_type=MESH,
        )

    def in_local(j, a):
        start = pl.multiple_of((me * PER + j) * HEAD, HEAD)
        return pltpu.make_async_copy(
            sources[a].at[0, 0, :, pl.ds(start, HEAD)], landing(j, a, me), in_recv.at[j, a, me]
        )

    def in_arrival(j, a, peer):
        return pltpu.make_async_remote_copy(
            src_ref=landing(j, a, peer),
            dst_ref=landing(j, a, peer),
            send_sem=in_send.at[j, a, peer],
            recv_sem=in_recv.at[j, a, peer],
            device_id=(peer, col),
            device_id_type=MESH,
        )

    def start_in(j, _):
        for a in range(4):
            for peer in (peers[1], peers[0], peers[2]):
                in_copy(j, a, peer).start()
            in_local(j, a).start()
        return 0

    lax.fori_loop(0, PER, start_in, 0)

    def wait_in(j, arrays):
        for a in arrays:
            in_local(j, a).wait()
            for peer in peers:
                in_arrival(j, a, peer).wait_recv()

    sides = ((0, has_low, -1), (1, has_high, 1))

    def kv_copy(j, side, step):
        return pltpu.make_async_remote_copy(
            src_ref=kv.at[j, 1],
            dst_ref=kv.at[j, 2 - 2 * side],
            send_sem=kv_send.at[j, side],
            recv_sem=kv_recv.at[j, 1 - side],
            device_id=(me, col + step),
            device_id_type=MESH,
        )

    def kv_arrival(j, side, step):
        return pltpu.make_async_remote_copy(
            src_ref=kv.at[j, 1],
            dst_ref=kv.at[j, 2 * side],
            send_sem=kv_send.at[j, side],
            recv_sem=kv_recv.at[j, side],
            device_id=(me, col + step),
            device_id_type=MESH,
        )

    def term_copy(j, side, step):
        return pltpu.make_async_remote_copy(
            src_ref=t_send.at[j, side],
            dst_ref=t_recv.at[j, 1 - side],
            send_sem=tr_send.at[j, side],
            recv_sem=tr_recv.at[j, 1 - side],
            device_id=(me, col + step),
            device_id_type=MESH,
        )

    def term_arrival(j, side, step):
        return pltpu.make_async_remote_copy(
            src_ref=t_send.at[j, side],
            dst_ref=t_recv.at[j, side],
            send_sem=tr_send.at[j, side],
            recv_sem=tr_recv.at[j, side],
            device_id=(me, col + step),
            device_id_type=MESH,
        )

    def forward(j):
        wait_in(j, (0, 1))
        for side, there, step in sides:

            @pl.when(there)
            def _():
                kv_copy(j, side, step).start()

            @pl.when(jnp.logical_not(there))
            def _():
                kv[j, 2 * side] = jnp.zeros((2, ROWS, TILE, HEAD), jnp.bfloat16)

    results = (dq_out, dk_out, dv_out)

    def out_place(j, o, row):
        start = pl.multiple_of((row * PER + j) * HEAD, HEAD)
        return results[o].at[0, 0, :, pl.ds(start, HEAD)]

    def out_copy(j, o, peer):
        return pltpu.make_async_remote_copy(
            src_ref=o_send.at[j, o, peer],
            dst_ref=out_place(j, o, me),
            send_sem=out_send.at[j, o, peer],
            recv_sem=out_recv.at[j, o, me],
            device_id=(peer, col),
            device_id_type=MESH,
        )

    def out_local(j, o):
        return pltpu.make_async_copy(
            o_send.at[j, o, me], out_place(j, o, me), out_send.at[j, o, me]
        )

    def out_arrival(j, o, peer):
        return pltpu.make_async_remote_copy(
            src_ref=o_send.at[j, o, peer],
            dst_ref=out_place(j, o, peer),
            send_sem=out_send.at[j, o, peer],
            recv_sem=out_recv.at[j, o, peer],
            device_id=(peer, col),
            device_id_type=MESH,
        )

    def start_out(j, o):
        for peer in (peers[1], peers[0], peers[2]):
            out_copy(j, o, peer).start()
        out_local(j, o).start()

    lane = lax.broadcasted_iota(jnp.int32, (1, 2 * TILE), 1)
    first_half = lane < TILE
    slot = lax.broadcasted_iota(jnp.int32, (TILE, 2 * TILE), 0)

    def visible_count(row, key_row, offset):
        there = col + offset - 1
        inside = (there >= 0) & (there < n_high)
        near = jnp.abs(row - key_row) <= 1
        same = clips[row] == clips[key_row]
        count = counts[key_row, jnp.clip(there, 0, n_high - 1)]
        return jnp.where(inside & near & same, count, 0)

    def fold(x, op):
        return op(x.reshape(TILE // 8, 8, 2 * TILE), axis=0)

    def block(j, b):
        row = 2 * b
        q = qg[j, 0, row : row + 2].reshape(2 * TILE, HEAD)
        g = qg[j, 1, row : row + 2].reshape(2 * TILE, HEAD)
        q_t = q.T
        g_t = g.T
        tiles = [(b + t // 3, t % 3) for t in range(WIN)]
        top = jnp.full((8, 2 * TILE), -1e30, jnp.float32)
        for t, (key_row, offset) in enumerate(tiles):
            s = jnp.dot(kv[j, offset, 0, key_row], q_t, preferred_element_type=jnp.float32)
            limit = jnp.where(
                first_half,
                visible_count(row, key_row, offset),
                visible_count(row + 1, key_row, offset),
            )
            s = jnp.where(slot < limit, s * (SCALE * math.log2(math.e)), jnp.float32(-1e30))
            score[t] = s
            top = jnp.maximum(top, fold(s, jnp.max))
            pgrad[t] = jnp.dot(kv[j, offset, 1, key_row], g_t, preferred_element_type=jnp.float32)
        top = jnp.max(top, axis=0, keepdims=True)
        total = jnp.zeros((8, 2 * TILE), jnp.float32)
        dot = jnp.zeros((8, 2 * TILE), jnp.float32)
        for t in range(WIN):
            e = jnp.exp2(score[t] - top)
            score[t] = e
            total = total + fold(e, jnp.sum)
            dot = dot + fold(e * pgrad[t], jnp.sum)
        total = jnp.sum(total, axis=0, keepdims=True)
        dot = jnp.sum(dot, axis=0, keepdims=True)
        own = jnp.where(first_half, counts[row, col], counts[row + 1, col] + TILE)
        inverse = 1.0 / total
        delta = dot * inverse
        inverse = jnp.where(lane < own, inverse, 0.0)
        for t, (key_row, offset) in enumerate(tiles):
            p = score[t] * inverse
            ds = (p * (pgrad[t] - delta)).astype(jnp.bfloat16)
            p = p.astype(jnp.bfloat16)
            k_t = kv[j, offset, 0, key_row].T
            dq = jnp.dot(k_t, ds, preferred_element_type=jnp.float32)
            dq_t[...] = dq if t == 0 else dq_t[...] + dq
            dk = jnp.dot(ds, q, preferred_element_type=jnp.float32)
            dv = jnp.dot(p, g, preferred_element_type=jnp.float32)
            if b > 0 and key_row < ROWS - 1:
                dk = dk + acc[j, offset, 0, key_row]
                dv = dv + acc[j, offset, 1, key_row]
            acc[j, offset, 0, key_row] = dk
            acc[j, offset, 1, key_row] = dv
        dq = (dq_t[...] * SCALE).T.astype(jnp.bfloat16)
        o_send[j, 0, row : row + 2] = dq.reshape(2, TILE, HEAD)

    def send_terms(j):
        for side, there, step in sides:

            @pl.when(there)
            def _():
                def cast(r, _):
                    t_send[j, side, 0, r] = (acc[j, 2 * side, 0, r] * SCALE).astype(jnp.bfloat16)
                    t_send[j, side, 1, r] = acc[j, 2 * side, 1, r].astype(jnp.bfloat16)
                    return 0

                lax.fori_loop(0, ROWS, cast, 0)
                term_copy(j, side, step).start()

    def finish(j):
        for side, there, step in sides:

            @pl.when(there)
            def _():
                term_arrival(j, side, step).wait_recv()

            @pl.when(jnp.logical_not(there))
            def _():
                t_recv[j, side] = jnp.zeros((2, ROWS, TILE, HEAD), jnp.bfloat16)

        def add(r, _):
            dk = (
                acc[j, 1, 0, r] * SCALE
                + t_recv[j, 0, 0, r].astype(jnp.float32)
                + t_recv[j, 1, 0, r].astype(jnp.float32)
            )
            dv = (
                acc[j, 1, 1, r]
                + t_recv[j, 0, 1, r].astype(jnp.float32)
                + t_recv[j, 1, 1, r].astype(jnp.float32)
            )
            o_send[j, 1, r] = dk.astype(jnp.bfloat16)
            o_send[j, 2, r] = dv.astype(jnp.bfloat16)
            return 0

        lax.fori_loop(0, ROWS, add, 0)
        start_out(j, 1)
        start_out(j, 2)

    forward(0)

    def head(j, _):
        @pl.when(j + 1 < PER)
        def _():
            forward(j + 1)

        wait_in(j, (2, 3))
        for side, there, step in sides:

            @pl.when(there)
            def _():
                kv_arrival(j, side, step).wait_recv()

        for b in range(ROWS // 2):
            block(j, b)

        send_terms(j)
        start_out(j, 0)

        @pl.when(j > 0)
        def _():
            finish(j - 1)

        return 0

    lax.fori_loop(0, PER, head, 0)
    finish(PER - 1)

    def drain(j, _):
        for a in range(4):
            for peer in peers:
                in_copy(j, a, peer).wait_send()
        for side, there, step in sides:

            @pl.when(there)
            def _():
                kv_copy(j, side, step).wait_send()
                term_copy(j, side, step).wait_send()

        for o in range(3):
            out_local(j, o).wait()
            for peer in peers:
                out_copy(j, o, peer).wait_send()
                out_arrival(j, o, peer).wait_recv()
        return 0

    lax.fori_loop(0, PER, drain, 0)


def by_heads(n_high, queries, keys, values, out_grad, tile_counts, clip_ids):
    tile = (TILE, HEAD)
    shape = jax.ShapeDtypeStruct(queries.shape, jnp.bfloat16)
    bf16, f32 = jnp.bfloat16, jnp.float32
    dma = pltpu.SemaphoreType.DMA
    pairs = 10 * 3 * PER
    return tuple(
        pl.pallas_call(
            functools.partial(head_kernel, n_high),
            out_shape=(shape, shape, shape),
            in_specs=[pl.BlockSpec(memory_space=pltpu.SMEM)] * 2
            + [pl.BlockSpec(memory_space=pltpu.HBM)] * 4,
            out_specs=(pl.BlockSpec(memory_space=pltpu.HBM),) * 3,
            scratch_shapes=[
                pltpu.VMEM((PER, 3, 2, ROWS) + tile, bf16),
                pltpu.VMEM((PER, 2, ROWS) + tile, bf16),
                pltpu.VMEM((WIN, TILE, 2 * TILE), f32),
                pltpu.VMEM((WIN, TILE, 2 * TILE), f32),
                pltpu.VMEM((HEAD, 2 * TILE), f32),
                pltpu.VMEM((PER, 3, 2, ROWS) + tile, f32),
                pltpu.VMEM((PER, 2, 2, ROWS) + tile, bf16),
                pltpu.VMEM((PER, 2, 2, ROWS) + tile, bf16),
                pltpu.VMEM((PER, 3, ROWS) + tile, bf16),
                dma((PER, 4, ROWS)),
                dma((PER, 4, ROWS)),
                dma((PER, 2)),
                dma((PER, 2)),
                dma((PER, 2)),
                dma((PER, 2)),
                dma((PER, 3, ROWS)),
                dma((PER, 3, ROWS)),
            ],
            compiler_params=pltpu.CompilerParams(
                collective_id=0, has_side_effects=True, vmem_limit_bytes=63 * 1024 * 1024
            ),
            cost_estimate=pl.CostEstimate(
                flops=pairs * 5 * 2 * TILE * TILE * HEAD,
                bytes_accessed=7 * TILE * HD * 2,
                transcendentals=pairs * TILE * TILE,
            ),
            name="head_parallel",
        )(tile_counts, clip_ids, queries, keys, values, out_grad)
    )


def extended(block, sides, width):
    for axis, dim in sides:
        count = lax.axis_size(axis)
        forward = [(i, i + 1) for i in range(count - 1)]
        backward = [(target, source) for source, target in forward]
        low = lax.ppermute(
            lax.slice_in_dim(block, block.shape[dim] - width, None, axis=dim), axis, forward
        )
        high = lax.ppermute(lax.slice_in_dim(block, 0, width, axis=dim), axis, backward)
        block = jnp.concatenate([low, block, high], axis=dim)
    return block


def window_mask(tile_counts, clip_ids, row, col):
    n_time = tile_counts.shape[0]
    n_high = tile_counts.shape[1]
    offsets = jnp.arange(3, dtype=jnp.int32) - 1
    along_t = row + offsets
    along_h = col + offsets
    inside = ((along_t >= 0) & (along_t < n_time))[:, None] & ((along_h >= 0) & (along_h < n_high))[
        None, :
    ]
    clamp_t = jnp.clip(along_t, 0, n_time - 1)
    clamp_h = jnp.clip(along_h, 0, n_high - 1)
    rows_all = jnp.arange(n_time, dtype=jnp.int32)
    cols_all = jnp.arange(n_high, dtype=jnp.int32)
    hits = (clamp_t[:, None, None, None] == rows_all[None, None, :, None]) & (
        clamp_h[None, :, None, None] == cols_all[None, None, None, :]
    )
    counts = jnp.sum(jnp.where(hits, tile_counts[None, None], 0), axis=(2, 3))
    clip_near = jnp.sum(
        jnp.where(clamp_t[:, None] == rows_all[None, :], clip_ids[None, :], 0), axis=1
    )
    same = clip_near == clip_near[1]
    slots = jnp.arange(TILE, dtype=jnp.int32)
    return inside[:, :, None] & same[:, None, None] & (slots[None, None, :] < counts[:, :, None])


def query_side(query, key_win, value_win, cotangent, key_mask, query_mask):
    scale = 1.0 / HEAD**0.5
    q_heads = query.reshape(TILE, HEADS, HEAD)
    k_heads = key_win.reshape(-1, HEADS, HEAD)
    v_heads = value_win.reshape(-1, HEADS, HEAD)
    g_heads = cotangent.reshape(TILE, HEADS, HEAD)
    scores = (
        jnp.einsum("qhd,khd->hqk", q_heads, k_heads, preferred_element_type=jnp.float32) * scale
    )
    scores = jnp.where(key_mask[None, None, :], scores, jnp.float32(-1e30))
    top = jnp.max(scores, axis=-1, keepdims=True)
    lse = top + jnp.log(jnp.sum(jnp.exp(scores - top), axis=-1, keepdims=True))
    probs = jnp.exp(scores - lse) * query_mask[None, :, None].astype(jnp.float32)
    probs_b = probs.astype(jnp.bfloat16)
    attended = jnp.einsum("hqk,khd->qhd", probs_b, v_heads, preferred_element_type=jnp.float32)
    delta = jnp.einsum("qhd,qhd->hq", g_heads.astype(jnp.float32), attended)
    prob_grad = jnp.einsum("qhd,khd->hqk", g_heads, v_heads, preferred_element_type=jnp.float32)
    score_grad = (probs * (prob_grad - delta[:, :, None])).astype(jnp.bfloat16)
    dquery = (
        jnp.einsum("hqk,khd->qhd", score_grad, k_heads, preferred_element_type=jnp.float32) * scale
    ).reshape(TILE, HD)
    dquery = dquery.astype(jnp.bfloat16)
    return (dquery, lse[:, :, 0], delta)


def local(queries, keys, values, out_grad, tile_counts, clip_ids):
    row = lax.axis_index("tm")
    col = lax.axis_index("height")
    visible = window_mask(tile_counts, clip_ids, row, col)
    own_mask = visible[1, 1]
    query = queries.reshape(TILE, HD)
    cotangent = out_grad.reshape(TILE, HD)
    windowed = extended(jnp.stack([keys, values]), (("tm", 1), ("height", 2)), 1)
    key_win = windowed[0].reshape(9 * TILE, HD)
    value_win = windowed[1].reshape(9 * TILE, HD)
    shape_out = (1, 1, TILE, HD)
    near = extended(jnp.stack([queries, out_grad]), (("tm", 1), ("height", 2)), 1)
    dquery, lse, delta = query_side(
        query, key_win, value_win, cotangent, visible.reshape(-1), own_mask
    )
    stats = extended(jnp.stack([lse, delta])[:, None, None], (("tm", 1), ("height", 2)), 1)
    lse_near = stats[0].transpose(2, 0, 1, 3).reshape(HEADS, 9 * TILE)
    delta_near = stats[1].transpose(2, 0, 1, 3).reshape(HEADS, 9 * TILE)
    scale = 1.0 / HEAD**0.5
    q_near = near[0].reshape(9 * TILE, HEADS, HEAD)
    g_near = near[1].reshape(9 * TILE, HEADS, HEAD)
    k_own = keys.reshape(TILE, HEADS, HEAD)
    v_own = values.reshape(TILE, HEADS, HEAD)
    pair_mask = visible.reshape(-1)[:, None] & own_mask[None, :]
    scores = jnp.einsum("qhd,khd->hqk", q_near, k_own, preferred_element_type=jnp.float32) * scale
    probs = jnp.where(pair_mask[None], jnp.exp(scores - lse_near[:, :, None]), jnp.float32(0.0))
    probs_b = probs.astype(jnp.bfloat16)
    prob_grad = jnp.einsum("qhd,khd->hqk", g_near, v_own, preferred_element_type=jnp.float32)
    score_grad = (probs * (prob_grad - delta_near[:, :, None])).astype(jnp.bfloat16)
    score_tiles = score_grad.reshape(HEADS, 9, TILE, TILE)
    probs_tiles = probs_b.reshape(HEADS, 9, TILE, TILE)
    q_tiles = q_near.reshape(9, TILE, HEADS, HEAD)
    g_tiles = g_near.reshape(9, TILE, HEADS, HEAD)
    key_terms = (
        jnp.einsum("hnqk,nqhd->nkhd", score_tiles, q_tiles, preferred_element_type=jnp.float32)
        * scale
    ).astype(jnp.bfloat16)
    value_terms = jnp.einsum(
        "hnqk,nqhd->nkhd", probs_tiles, g_tiles, preferred_element_type=jnp.float32
    ).astype(jnp.bfloat16)
    dkey = jnp.sum(key_terms.astype(jnp.float32), axis=0)
    dvalue = jnp.sum(value_terms.astype(jnp.float32), axis=0)
    key_grad = dkey.reshape(shape_out).astype(jnp.bfloat16)
    value_grad = dvalue.reshape(shape_out).astype(jnp.bfloat16)
    return (dquery.reshape(shape_out), key_grad, value_grad)


def solution(mesh):
    placed = (
        P("tm", "height", None, None),
        P("tm", "height", None, None),
        P("tm", "height", None, None),
        P("tm", "height", None, None),
        P(),
        P(),
    )
    if mesh.shape["tm"] == ROWS:
        body = functools.partial(by_heads, mesh.shape["height"])
    else:
        body = local
    return jax.shard_map(
        body,
        mesh=mesh,
        in_specs=placed,
        out_specs=(
            P("tm", "height", None, None),
            P("tm", "height", None, None),
            P("tm", "height", None, None),
        ),
        check_vma=False,
    )
```

```python
import functools
import math

import jax
import jax.numpy as jnp
from jax import lax
from jax.experimental import pallas as pl
from jax.experimental.pallas import tpu as pltpu
from jax.sharding import PartitionSpec as P

HEADS = 12
HEAD = 128
TILE = 192
HD = 1536
MESH = pl.DeviceIdType.MESH
SCALE = 1.0 / HEAD**0.5
ROWS = 4
PER = HEADS // ROWS
PIECES = 2
WIN = 9


def head_kernel(
    n_high,
    counts_in,
    clips_in,
    q_in,
    k_in,
    v_in,
    g_in,
    dq_out,
    dk_out,
    dv_out,
    kv,
    qg,
    score,
    pgrad,
    dq_t,
    acc,
    t_send,
    t_recv,
    o_send,
    counts,
    clips,
    small,
    in_send,
    in_recv,
    kv_send,
    kv_recv,
    tr_send,
    tr_recv,
    out_send,
    out_recv,
):
    me = lax.axis_index("tm")
    col = lax.axis_index("height")
    has_low = col > 0
    has_high = col < n_high - 1
    peers = [lax.rem(me + i, ROWS) for i in (1, 2, 3)]

    small_copies = (
        pltpu.make_async_copy(counts_in, counts, small.at[0]),
        pltpu.make_async_copy(clips_in, clips, small.at[1]),
    )
    for copy in small_copies:
        copy.start()

    barrier = pltpu.get_barrier_semaphore()
    for peer in peers:
        pl.semaphore_signal(barrier, inc=1, device_id=(peer, col), device_id_type=MESH)

    @pl.when(has_low)
    def _():
        pl.semaphore_signal(barrier, inc=1, device_id=(me, col - 1), device_id_type=MESH)

    @pl.when(has_high)
    def _():
        pl.semaphore_signal(barrier, inc=1, device_id=(me, col + 1), device_id_type=MESH)

    pl.semaphore_wait(barrier, 3 + has_low.astype(jnp.int32) + has_high.astype(jnp.int32))

    sources = (k_in, v_in, q_in, g_in)

    def landing(j, a, r):
        return kv.at[j, 1, a, r] if a < 2 else qg.at[j, a - 2, r]

    def in_copy(j, a, peer):
        start = pl.multiple_of((peer * PER + j) * HEAD, HEAD)
        return pltpu.make_async_remote_copy(
            src_ref=sources[a].at[0, 0, :, pl.ds(start, HEAD)],
            dst_ref=landing(j, a, me),
            send_sem=in_send.at[j, a, peer],
            recv_sem=in_recv.at[j, a, me],
            device_id=(peer, col),
            device_id_type=MESH,
        )

    def in_local(j, a):
        start = pl.multiple_of((me * PER + j) * HEAD, HEAD)
        return pltpu.make_async_copy(
            sources[a].at[0, 0, :, pl.ds(start, HEAD)], landing(j, a, me), in_recv.at[j, a, me]
        )

    def in_arrival(j, a, peer):
        return pltpu.make_async_remote_copy(
            src_ref=landing(j, a, peer),
            dst_ref=landing(j, a, peer),
            send_sem=in_send.at[j, a, peer],
            recv_sem=in_recv.at[j, a, peer],
            device_id=(peer, col),
            device_id_type=MESH,
        )

    def start_in(j, _):
        for a in range(4):
            for peer in (peers[1], peers[0], peers[2]):
                in_copy(j, a, peer).start()
            in_local(j, a).start()
        return 0

    lax.fori_loop(0, PER, start_in, 0)

    def wait_in(j, arrays):
        for a in arrays:
            in_local(j, a).wait()
            for peer in peers:
                in_arrival(j, a, peer).wait_recv()

    sides = ((0, has_low, -1), (1, has_high, 1))

    def kv_copy(j, side, step):
        return pltpu.make_async_remote_copy(
            src_ref=kv.at[j, 1],
            dst_ref=kv.at[j, 2 - 2 * side],
            send_sem=kv_send.at[j, side],
            recv_sem=kv_recv.at[j, 1 - side],
            device_id=(me, col + step),
            device_id_type=MESH,
        )

    def kv_arrival(j, side, step):
        return pltpu.make_async_remote_copy(
            src_ref=kv.at[j, 1],
            dst_ref=kv.at[j, 2 * side],
            send_sem=kv_send.at[j, side],
            recv_sem=kv_recv.at[j, side],
            device_id=(me, col + step),
            device_id_type=MESH,
        )

    def term_copy(j, side, step):
        return pltpu.make_async_remote_copy(
            src_ref=t_send.at[j, side],
            dst_ref=t_recv.at[j, 1 - side],
            send_sem=tr_send.at[j, side],
            recv_sem=tr_recv.at[j, 1 - side],
            device_id=(me, col + step),
            device_id_type=MESH,
        )

    def term_arrival(j, side, step):
        return pltpu.make_async_remote_copy(
            src_ref=t_send.at[j, side],
            dst_ref=t_recv.at[j, side],
            send_sem=tr_send.at[j, side],
            recv_sem=tr_recv.at[j, side],
            device_id=(me, col + step),
            device_id_type=MESH,
        )

    def forward(j):
        wait_in(j, (0, 1))
        for side, there, step in sides:

            @pl.when(there)
            def _():
                kv_copy(j, side, step).start()

            @pl.when(jnp.logical_not(there))
            def _():
                kv[j, 2 * side] = jnp.zeros((2, ROWS, TILE, HEAD), jnp.bfloat16)

    results = (dq_out, dk_out, dv_out)

    def out_place(j, o, row):
        start = pl.multiple_of((row * PER + j) * HEAD, HEAD)
        return results[o].at[0, 0, :, pl.ds(start, HEAD)]

    def out_copy(j, o, peer):
        return pltpu.make_async_remote_copy(
            src_ref=o_send.at[j, o, peer],
            dst_ref=out_place(j, o, me),
            send_sem=out_send.at[j, o, peer],
            recv_sem=out_recv.at[j, o, me],
            device_id=(peer, col),
            device_id_type=MESH,
        )

    def out_local(j, o):
        return pltpu.make_async_copy(
            o_send.at[j, o, me], out_place(j, o, me), out_send.at[j, o, me]
        )

    def out_arrival(j, o, peer):
        return pltpu.make_async_remote_copy(
            src_ref=o_send.at[j, o, peer],
            dst_ref=out_place(j, o, peer),
            send_sem=out_send.at[j, o, peer],
            recv_sem=out_recv.at[j, o, peer],
            device_id=(peer, col),
            device_id_type=MESH,
        )

    def start_out(j, o):
        for peer in (peers[1], peers[0], peers[2]):
            out_copy(j, o, peer).start()
        out_local(j, o).start()

    lane = lax.broadcasted_iota(jnp.int32, (1, 2 * TILE), 1)
    first_half = lane < TILE
    slot = lax.broadcasted_iota(jnp.int32, (TILE, 2 * TILE), 0)

    def visible_count(row, key_row, offset):
        there = col + offset - 1
        inside = (there >= 0) & (there < n_high)
        near = jnp.abs(row - key_row) <= 1
        same = clips[row] == clips[key_row]
        count = counts[key_row, jnp.clip(there, 0, n_high - 1)]
        return jnp.where(inside & near & same, count, 0)

    def fold(x, op):
        return op(x.reshape(TILE // 8, 8, 2 * TILE), axis=0)

    def send_terms(j, which):
        side, there, step = sides[which]

        @pl.when(there)
        def _():
            for r in range(ROWS):
                t_send[j, side, 0, r] = (acc[j, 2 * side, 0, r] * SCALE).astype(jnp.bfloat16)
                t_send[j, side, 1, r] = acc[j, 2 * side, 1, r].astype(jnp.bfloat16)
            term_copy(j, side, step).start()

    def block(j, b):
        row = 2 * b
        q = qg[j, 0, row : row + 2].reshape(2 * TILE, HEAD)
        g = qg[j, 1, row : row + 2].reshape(2 * TILE, HEAD)
        q_t = q.T
        g_t = g.T
        tiles = [(b + t % 3, (0, 2, 1)[t // 3]) for t in range(WIN)]
        top = jnp.full((8, 2 * TILE), -1e30, jnp.float32)
        for t, (key_row, offset) in enumerate(tiles):
            s = jnp.dot(kv[j, offset, 0, key_row], q_t, preferred_element_type=jnp.float32)
            limit = jnp.where(
                first_half,
                visible_count(row, key_row, offset),
                visible_count(row + 1, key_row, offset),
            )
            s = jnp.where(slot < limit, s * (SCALE * math.log2(math.e)), jnp.float32(-1e30))
            score[t] = s
            top = jnp.maximum(top, fold(s, jnp.max))
            pgrad[t] = jnp.dot(kv[j, offset, 1, key_row], g_t, preferred_element_type=jnp.float32)
        top = jnp.max(top, axis=0, keepdims=True)
        total = jnp.zeros((8, 2 * TILE), jnp.float32)
        dot = jnp.zeros((8, 2 * TILE), jnp.float32)
        for t in range(WIN):
            e = jnp.exp2(score[t] - top)
            score[t] = e
            total = total + fold(e, jnp.sum)
            dot = dot + fold(e * pgrad[t], jnp.sum)
        total = jnp.sum(total, axis=0, keepdims=True)
        dot = jnp.sum(dot, axis=0, keepdims=True)
        own = jnp.where(first_half, counts[row, col], counts[row + 1, col] + TILE)
        inverse = 1.0 / total
        delta = dot * inverse
        inverse = jnp.where(lane < own, inverse, 0.0)
        for t, (key_row, offset) in enumerate(tiles):
            p = score[t] * inverse
            ds = (p * (pgrad[t] - delta)).astype(jnp.bfloat16)
            p = p.astype(jnp.bfloat16)
            k_t = kv[j, offset, 0, key_row].T
            dq = jnp.dot(k_t, ds, preferred_element_type=jnp.float32)
            dq_t[...] = dq if t == 0 else dq_t[...] + dq
            dk = jnp.dot(ds, q, preferred_element_type=jnp.float32)
            dv = jnp.dot(p, g, preferred_element_type=jnp.float32)
            if b > 0 and key_row < ROWS - 1:
                dk = dk + acc[j, offset, 0, key_row]
                dv = dv + acc[j, offset, 1, key_row]
            acc[j, offset, 0, key_row] = dk
            acc[j, offset, 1, key_row] = dv
            if b == ROWS // 2 - 1 and t in (2, 5):
                send_terms(j, t // 5)
        dq = (dq_t[...] * SCALE).T.astype(jnp.bfloat16)
        o_send[j, 0, row : row + 2] = dq.reshape(2, TILE, HEAD)

    def finish(j):
        for side, there, step in sides:

            @pl.when(there)
            def _():
                term_arrival(j, side, step).wait_recv()

            @pl.when(jnp.logical_not(there))
            def _():
                t_recv[j, side] = jnp.zeros((2, ROWS, TILE, HEAD), jnp.bfloat16)

        def add(r, _):
            dk = (
                acc[j, 1, 0, r] * SCALE
                + t_recv[j, 0, 0, r].astype(jnp.float32)
                + t_recv[j, 1, 0, r].astype(jnp.float32)
            )
            dv = (
                acc[j, 1, 1, r]
                + t_recv[j, 0, 1, r].astype(jnp.float32)
                + t_recv[j, 1, 1, r].astype(jnp.float32)
            )
            o_send[j, 1, r] = dk.astype(jnp.bfloat16)
            o_send[j, 2, r] = dv.astype(jnp.bfloat16)
            return 0

        lax.fori_loop(0, ROWS, add, 0)
        start_out(j, 1)
        start_out(j, 2)

    for copy in small_copies:
        copy.wait()

    forward(0)

    def head(j, _):
        @pl.when(j + 1 < PER)
        def _():
            forward(j + 1)

        wait_in(j, (2, 3))
        for side, there, step in sides:

            @pl.when(there)
            def _():
                kv_arrival(j, side, step).wait_recv()

        for b in range(ROWS // 2):
            block(j, b)

        start_out(j, 0)

        @pl.when(j > 0)
        def _():
            finish(j - 1)

        return 0

    lax.fori_loop(0, PER, head, 0)
    finish(PER - 1)

    def drain(j, _):
        for a in range(4):
            for peer in peers:
                in_copy(j, a, peer).wait_send()
        for side, there, step in sides:

            @pl.when(there)
            def _():
                kv_copy(j, side, step).wait_send()
                term_copy(j, side, step).wait_send()

        for o in range(3):
            out_local(j, o).wait()
            for peer in peers:
                out_copy(j, o, peer).wait_send()
                out_arrival(j, o, peer).wait_recv()
        return 0

    lax.fori_loop(0, PER, drain, 0)


def place_kernel(dq, dk, dv, dq_out, dk_out, dv_out, held, sem):
    rows = TILE // PIECES
    copies = [
        (
            pltpu.make_async_copy(
                source.at[0, 0, pl.ds(i * rows, rows)], held.at[a, i], sem.at[0, a, i]
            ),
            pltpu.make_async_copy(
                held.at[a, i], target.at[0, 0, pl.ds(i * rows, rows)], sem.at[1, a, i]
            ),
        )
        for a, (source, target) in enumerate(((dq, dq_out), (dk, dk_out), (dv, dv_out)))
        for i in range(PIECES)
    ]
    for arrive, _ in copies:
        arrive.start()
    for arrive, leave in copies:
        arrive.wait()
        leave.start()
    for _, leave in copies:
        leave.wait()


def by_heads(n_high, queries, keys, values, out_grad, tile_counts, clip_ids):
    tile = (TILE, HEAD)
    shape = jax.ShapeDtypeStruct(queries.shape, jnp.bfloat16)
    bf16, f32 = jnp.bfloat16, jnp.float32
    dma = pltpu.SemaphoreType.DMA
    pairs = 10 * 3 * PER
    parts = (
        pl.pallas_call(
            functools.partial(head_kernel, n_high),
            out_shape=(shape, shape, shape),
            in_specs=[pl.BlockSpec(memory_space=pltpu.HBM)] * 6,
            out_specs=(pl.BlockSpec(memory_space=pltpu.HBM),) * 3,
            scratch_shapes=[
                pltpu.VMEM((PER, 3, 2, ROWS) + tile, bf16),
                pltpu.VMEM((PER, 2, ROWS) + tile, bf16),
                pltpu.VMEM((WIN, TILE, 2 * TILE), f32),
                pltpu.VMEM((WIN, TILE, 2 * TILE), f32),
                pltpu.VMEM((HEAD, 2 * TILE), f32),
                pltpu.VMEM((PER, 3, 2, ROWS) + tile, f32),
                pltpu.VMEM((PER, 2, 2, ROWS) + tile, bf16),
                pltpu.VMEM((PER, 2, 2, ROWS) + tile, bf16),
                pltpu.VMEM((PER, 3, ROWS) + tile, bf16),
                pltpu.SMEM(tile_counts.shape, jnp.int32),
                pltpu.SMEM(clip_ids.shape, jnp.int32),
                dma((2,)),
                dma((PER, 4, ROWS)),
                dma((PER, 4, ROWS)),
                dma((PER, 2)),
                dma((PER, 2)),
                dma((PER, 2)),
                dma((PER, 2)),
                dma((PER, 3, ROWS)),
                dma((PER, 3, ROWS)),
            ],
            compiler_params=pltpu.CompilerParams(
                collective_id=0, has_side_effects=True, vmem_limit_bytes=63 * 1024 * 1024
            ),
            cost_estimate=pl.CostEstimate(
                flops=pairs * 5 * 2 * TILE * TILE * HEAD,
                bytes_accessed=7 * TILE * HD * 2,
                transcendentals=pairs * TILE * TILE,
            ),
            name="head_parallel",
        )(tile_counts, clip_ids, queries, keys, values, out_grad)
    )
    return tuple(
        pl.pallas_call(
            place_kernel,
            out_shape=(shape, shape, shape),
            in_specs=[pl.BlockSpec(memory_space=pl.ANY)] * 3,
            out_specs=(pl.BlockSpec(memory_space=pl.ANY),) * 3,
            scratch_shapes=[
                pltpu.VMEM((3, PIECES, TILE // PIECES, HD), bf16),
                dma((2, 3, PIECES)),
            ],
            cost_estimate=pl.CostEstimate(
                flops=0, bytes_accessed=6 * TILE * HD * 2, transcendentals=0
            ),
            name="place",
        )(*parts)
    )


def extended(block, sides, width):
    for axis, dim in sides:
        count = lax.axis_size(axis)
        forward = [(i, i + 1) for i in range(count - 1)]
        backward = [(target, source) for source, target in forward]
        low = lax.ppermute(
            lax.slice_in_dim(block, block.shape[dim] - width, None, axis=dim), axis, forward
        )
        high = lax.ppermute(lax.slice_in_dim(block, 0, width, axis=dim), axis, backward)
        block = jnp.concatenate([low, block, high], axis=dim)
    return block


def window_mask(tile_counts, clip_ids, row, col):
    n_time = tile_counts.shape[0]
    n_high = tile_counts.shape[1]
    offsets = jnp.arange(3, dtype=jnp.int32) - 1
    along_t = row + offsets
    along_h = col + offsets
    inside = ((along_t >= 0) & (along_t < n_time))[:, None] & ((along_h >= 0) & (along_h < n_high))[
        None, :
    ]
    clamp_t = jnp.clip(along_t, 0, n_time - 1)
    clamp_h = jnp.clip(along_h, 0, n_high - 1)
    rows_all = jnp.arange(n_time, dtype=jnp.int32)
    cols_all = jnp.arange(n_high, dtype=jnp.int32)
    hits = (clamp_t[:, None, None, None] == rows_all[None, None, :, None]) & (
        clamp_h[None, :, None, None] == cols_all[None, None, None, :]
    )
    counts = jnp.sum(jnp.where(hits, tile_counts[None, None], 0), axis=(2, 3))
    clip_near = jnp.sum(
        jnp.where(clamp_t[:, None] == rows_all[None, :], clip_ids[None, :], 0), axis=1
    )
    same = clip_near == clip_near[1]
    slots = jnp.arange(TILE, dtype=jnp.int32)
    return inside[:, :, None] & same[:, None, None] & (slots[None, None, :] < counts[:, :, None])


def query_side(query, key_win, value_win, cotangent, key_mask, query_mask):
    scale = 1.0 / HEAD**0.5
    q_heads = query.reshape(TILE, HEADS, HEAD)
    k_heads = key_win.reshape(-1, HEADS, HEAD)
    v_heads = value_win.reshape(-1, HEADS, HEAD)
    g_heads = cotangent.reshape(TILE, HEADS, HEAD)
    scores = (
        jnp.einsum("qhd,khd->hqk", q_heads, k_heads, preferred_element_type=jnp.float32) * scale
    )
    scores = jnp.where(key_mask[None, None, :], scores, jnp.float32(-1e30))
    top = jnp.max(scores, axis=-1, keepdims=True)
    lse = top + jnp.log(jnp.sum(jnp.exp(scores - top), axis=-1, keepdims=True))
    probs = jnp.exp(scores - lse) * query_mask[None, :, None].astype(jnp.float32)
    probs_b = probs.astype(jnp.bfloat16)
    attended = jnp.einsum("hqk,khd->qhd", probs_b, v_heads, preferred_element_type=jnp.float32)
    delta = jnp.einsum("qhd,qhd->hq", g_heads.astype(jnp.float32), attended)
    prob_grad = jnp.einsum("qhd,khd->hqk", g_heads, v_heads, preferred_element_type=jnp.float32)
    score_grad = (probs * (prob_grad - delta[:, :, None])).astype(jnp.bfloat16)
    dquery = (
        jnp.einsum("hqk,khd->qhd", score_grad, k_heads, preferred_element_type=jnp.float32) * scale
    ).reshape(TILE, HD)
    dquery = dquery.astype(jnp.bfloat16)
    return (dquery, lse[:, :, 0], delta)


def local(queries, keys, values, out_grad, tile_counts, clip_ids):
    row = lax.axis_index("tm")
    col = lax.axis_index("height")
    visible = window_mask(tile_counts, clip_ids, row, col)
    own_mask = visible[1, 1]
    query = queries.reshape(TILE, HD)
    cotangent = out_grad.reshape(TILE, HD)
    windowed = extended(jnp.stack([keys, values]), (("tm", 1), ("height", 2)), 1)
    key_win = windowed[0].reshape(9 * TILE, HD)
    value_win = windowed[1].reshape(9 * TILE, HD)
    shape_out = (1, 1, TILE, HD)
    near = extended(jnp.stack([queries, out_grad]), (("tm", 1), ("height", 2)), 1)
    dquery, lse, delta = query_side(
        query, key_win, value_win, cotangent, visible.reshape(-1), own_mask
    )
    stats = extended(jnp.stack([lse, delta])[:, None, None], (("tm", 1), ("height", 2)), 1)
    lse_near = stats[0].transpose(2, 0, 1, 3).reshape(HEADS, 9 * TILE)
    delta_near = stats[1].transpose(2, 0, 1, 3).reshape(HEADS, 9 * TILE)
    scale = 1.0 / HEAD**0.5
    q_near = near[0].reshape(9 * TILE, HEADS, HEAD)
    g_near = near[1].reshape(9 * TILE, HEADS, HEAD)
    k_own = keys.reshape(TILE, HEADS, HEAD)
    v_own = values.reshape(TILE, HEADS, HEAD)
    pair_mask = visible.reshape(-1)[:, None] & own_mask[None, :]
    scores = jnp.einsum("qhd,khd->hqk", q_near, k_own, preferred_element_type=jnp.float32) * scale
    probs = jnp.where(pair_mask[None], jnp.exp(scores - lse_near[:, :, None]), jnp.float32(0.0))
    probs_b = probs.astype(jnp.bfloat16)
    prob_grad = jnp.einsum("qhd,khd->hqk", g_near, v_own, preferred_element_type=jnp.float32)
    score_grad = (probs * (prob_grad - delta_near[:, :, None])).astype(jnp.bfloat16)
    score_tiles = score_grad.reshape(HEADS, 9, TILE, TILE)
    probs_tiles = probs_b.reshape(HEADS, 9, TILE, TILE)
    q_tiles = q_near.reshape(9, TILE, HEADS, HEAD)
    g_tiles = g_near.reshape(9, TILE, HEADS, HEAD)
    key_terms = (
        jnp.einsum("hnqk,nqhd->nkhd", score_tiles, q_tiles, preferred_element_type=jnp.float32)
        * scale
    ).astype(jnp.bfloat16)
    value_terms = jnp.einsum(
        "hnqk,nqhd->nkhd", probs_tiles, g_tiles, preferred_element_type=jnp.float32
    ).astype(jnp.bfloat16)
    dkey = jnp.sum(key_terms.astype(jnp.float32), axis=0)
    dvalue = jnp.sum(value_terms.astype(jnp.float32), axis=0)
    key_grad = dkey.reshape(shape_out).astype(jnp.bfloat16)
    value_grad = dvalue.reshape(shape_out).astype(jnp.bfloat16)
    return (dquery.reshape(shape_out), key_grad, value_grad)


def solution(mesh):
    placed = (
        P("tm", "height", None, None),
        P("tm", "height", None, None),
        P("tm", "height", None, None),
        P("tm", "height", None, None),
        P(),
        P(),
    )
    if mesh.shape["tm"] == ROWS:
        body = functools.partial(by_heads, mesh.shape["height"])
    else:
        body = local
    return jax.shard_map(
        body,
        mesh=mesh,
        in_specs=placed,
        out_specs=(
            P("tm", "height", None, None),
            P("tm", "height", None, None),
            P("tm", "height", None, None),
        ),
        check_vma=False,
    )
```
